512 devices in a mesh: dp: 2 (over core), row: 16 (over z, x_hi), col: 16 (over x_lo, y).
Axes of the slice: x: 4 (x_hi: 2, x_lo: 2; x = x_hi * 2 + x_lo), y: 8, z: 8, core: 2. Of those that a mesh axis runs over, the one named last changes fastest.
Arguments:
- tokens: bfloat16 [512, 12288], P(('dp', 'col'), 'row'), may hold values from -6 to 6
- w_up: bfloat16 [12288, 24576], P('row', ('dp', 'col')), may hold values from -0.0546875 to 0.0546875
- w_down: bfloat16 [24576, 12288], P(('dp', 'col'), 'row'), may hold values from -0.0390625 to 0.0390625
- grad_out: bfloat16 [512, 12288], P(('dp', 'col'), 'row'), may hold values from -6 to 6
Outputs:
- grad_tokens: bfloat16 [512, 12288], P(('dp', 'col'), 'row')
- grad_w_up: bfloat16 [12288, 24576], P('row', ('dp', 'col'))
- grad_w_down: bfloat16 [24576, 12288], P(('dp', 'col'), 'row')
The draws below stay inside these ranges and needn't reach their ends.
All inputs are finite; a program needn't handle non-finite values.
Results may differ from the reference program's by a relative error of at most 0.0049.
Values may be sent and summed in bfloat16 or wider, within the bound.
A program may use at most 64 MiB of HBM per device.

```python
import math
import jax
import jax.numpy as jnp

D = 12288
FF = 24576
TOKENS = 512


def block_levels(rng, shape, cuts, least, top_value):
    gain = 1.0
    for position, blocks in cuts:
        draws = jax.random.uniform(jax.random.fold_in(jax.random.fold_in(rng, 6), position), (blocks,), jnp.float32, least / len(cuts), top_value / len(cuts))
        gain = gain * jnp.repeat(jnp.exp(draws), shape[position] // blocks).reshape((-1,) + (1,) * (len(shape) - 1 - position))
    return gain


def normal_values(own_key, dims, scale, reach, cuts=(), kind=jnp.bfloat16):
    entries = jax.random.normal(own_key, dims, jnp.float32) * scale
    if len(cuts) > 0:
        entries = block_levels(own_key, dims, cuts, -0.22, 0.18) * entries
    return jnp.clip(entries, min=-reach, max=reach).astype(kind)


def setup_inputs(seed: int = 0) -> dict:
    key_list = jax.random.split(jax.random.key(seed), 5)
    tokens = normal_values(key_list[0], (TOKENS, D), 1.0, 6.0, ((0, 32), (1, 16)))
    w_up = normal_values(key_list[1], (D, FF), D ** -0.5, 0.0546875, ((0, 16), (1, 32)))
    w_down = normal_values(key_list[2], (FF, D), FF ** -0.5, 0.0390625, ((0, 32), (1, 16)))
    grad_out = normal_values(key_list[3], (TOKENS, D), 1.0, 6.0, ((0, 32), (1, 16)))
    return {"tokens": tokens, "w_up": w_up, "w_down": w_down, "grad_out": grad_out}


slope_c = math.sqrt(2.0 / math.pi)
cubic_a = 0.044715

def gelu_value(u):
    t = jnp.tanh(slope_c * (u + cubic_a * u * u * u))
    return 0.5 * u * (1.0 + t)

def gelu_slope(u):
    t = jnp.tanh(slope_c * (u + cubic_a * u * u * u))
    return 0.5 * (1.0 + t) + 0.5 * u * (1.0 - t * t) * slope_c * (1.0 + 3.0 * cubic_a * u * u)

def reference(tokens, w_up, w_down, grad_out):
    pre = jnp.dot(tokens, w_up, preferred_element_type=jnp.float32)
    act = gelu_value(pre).astype(jnp.bfloat16)
    grad_act = jnp.dot(grad_out, w_down.T, preferred_element_type=jnp.float32)
    grad_pre = (grad_act * gelu_slope(pre)).astype(jnp.bfloat16)
    grad_w_down = jnp.dot(act.T, grad_out, preferred_element_type=jnp.float32).astype(jnp.bfloat16)
    grad_w_up = jnp.dot(tokens.T, grad_pre, preferred_element_type=jnp.float32).astype(jnp.bfloat16)
    grad_tokens = jnp.dot(grad_pre, w_up.T, preferred_element_type=jnp.float32).astype(jnp.bfloat16)
    return (grad_tokens, grad_w_up, grad_w_down)
```

```python
import functools
import math

import jax
import jax.numpy as jnp
from jax import lax
from jax.experimental import pallas as pl
from jax.experimental.pallas import tpu as pltpu
from jax.sharding import PartitionSpec as P

slope_c = math.sqrt(2.0 / math.pi)
cubic_a = 0.044715
f32 = jnp.float32
bf16 = jnp.bfloat16
tile = 16


def dot_plain(left, right):
    return lax.dot_general(left, right, (((1,), (0,)), ((), ())), preferred_element_type=f32)


def dot_right_t(left, right):
    return lax.dot_general(left, right, (((1,), (1,)), ((), ())), preferred_element_type=f32)


def dot_left_t(left, right):
    return lax.dot_general(left, right, (((0,), (0,)), ((), ())), preferred_element_type=f32)


def remote(src, dst, send_sem, recv_sem, device):
    return pltpu.make_async_remote_copy(
        src_ref=src,
        dst_ref=dst,
        send_sem=send_sem,
        recv_sem=recv_sem,
        device_id=device,
        device_id_type=pl.DeviceIdType.MESH,
    )


class Ring:
    def __init__(self, place, size, up, down, ups, downs, send_sems, recv_sems, sent):
        self.place, self.size, self.sent = place, size, sent
        self.ways = ((1, ups, 0, up), (-1, downs, ups, down))
        self.send_sems, self.recv_sems = send_sems, recv_sems

    def at(self, offset):
        return lax.rem(self.place + (offset + self.size), self.size)


class Gather(Ring):
    def copy(self, way, step, view, received=False):
        sign, _, base, device = way
        q = self.at(-sign * (step + 1 if received else step))
        ref = view(q)
        slot = base + step
        return remote(ref, ref, self.send_sems.at[slot], self.recv_sems.at[slot], device)

    def send(self, step, view):
        for way in self.ways:
            if step < way[1]:
                copy = self.copy(way, step, view)
                copy.start()
                self.sent.append(copy)

    def arrive(self, step, view):
        here = []
        for way in self.ways:
            if step < way[1]:
                self.copy(way, step, view, received=True).wait_recv()
                here.append(self.at(-way[0] * (step + 1)))
        return here


class Scatter(Ring):
    def bind(self, part, out_slots, in_slots):
        self.part, self.out_slots, self.in_slots = part, out_slots, in_slots
        return self

    def copy(self, way, step):
        _, _, base, device = way
        slot = base + step
        return remote(
            self.out_slots.at[slot],
            self.in_slots.at[slot],
            self.send_sems.at[slot],
            self.recv_sems.at[slot],
            device,
        )

    def step(self, step):
        for way in self.ways:
            sign, hops, base, _ = way
            if step < hops:
                total = self.part(self.at(sign * (hops - step)))
                if step > 0:
                    self.copy(way, step - 1).wait_recv()
                    total = total + self.in_slots[base + step - 1].astype(f32)
                self.out_slots[base + step] = total.astype(self.out_slots.dtype)
                copy = self.copy(way, step)
                copy.start()
                self.sent.append(copy)

    def finish(self):
        total = self.part(self.place)
        for way in self.ways:
            _, hops, base, _ = way
            if hops > 0:
                self.copy(way, hops - 1).wait_recv()
                total = total + self.in_slots[base + hops - 1].astype(f32)
        return total


def kernel(
    nz, ny,
    x_in, wu_in, wd_in, dy_in,
    gin_out, gu_out, gd_out,
    xg, dyg, wu, wd, pre_p, gact_p,
    pre_out, pre_in, gact_out, gact_in,
    pair_out, pair_in, slope,
    act, gpre, gin_p, sib_out, sib_in, gin_o, gin_i, last_out, last_in, gu, gd,
    local_sem, xlo_s, xlo_r, y_s, y_r, sib_s, sib_r, z_s, z_r, pair_s, pair_r,
    gsib_s, gsib_r, gy_s, gy_r, gx_s, gx_r,
):
    core = lax.axis_index("dp")
    row = lax.axis_index("row")
    col = lax.axis_index("col")
    z, x_hi = lax.div(row, 2), lax.rem(row, 2)
    x_lo, y = lax.div(col, ny), lax.rem(col, ny)
    sent = []

    def start(copy):
        copy.start()
        sent.append(copy)

    z_up = {"row": lax.rem(z + 1, nz) * 2 + x_hi}
    z_down = {"row": lax.rem(z + nz - 1, nz) * 2 + x_hi}
    far = {"row": z * 2 + (1 - x_hi)}
    y_up = {"col": x_lo * ny + lax.rem(y + 1, ny)}
    y_down = {"col": x_lo * ny + lax.rem(y + ny - 1, ny)}
    near = {"col": (1 - x_lo) * ny + y}
    sibling = {"dp": 1 - core}

    mine = pl.ds(pl.multiple_of(core * (2 * tile), 2 * tile), 2 * tile)
    theirs = pl.ds(pl.multiple_of((1 - core) * (2 * tile), 2 * tile), 2 * tile)
    own_tile = pl.ds(pl.multiple_of(core * (2 * tile) + x_lo * tile, tile), tile)
    near_tile = pl.ds(pl.multiple_of(core * (2 * tile) + (1 - x_lo) * tile, tile), tile)

    fetch_x = pltpu.make_async_copy(x_in, xg.at[y, own_tile], local_sem.at[0])
    fetch_dy = pltpu.make_async_copy(dy_in, dyg.at[y, own_tile], local_sem.at[1])
    fetch_wu = pltpu.make_async_copy(wu_in, wu, local_sem.at[2])
    fetch_wd = pltpu.make_async_copy(wd_in, wd, local_sem.at[3])
    for copy in (fetch_x, fetch_dy, fetch_wu, fetch_wd):
        copy.start()

    barrier = pltpu.get_barrier_semaphore()
    others = (z_up, z_down, far, y_up, y_down, near, sibling)
    for device in others:
        pl.semaphore_signal(barrier, inc=1, device_id=device, device_id_type=pl.DeviceIdType.MESH)
    pl.semaphore_wait(barrier, len(others))

    y_long, y_short = ny // 2, ny - 1 - ny // 2
    z_long, z_short = nz // 2, nz - 1 - nz // 2
    y_steps, z_steps = ny - 1, nz - 1

    def near_copy(i, ref, rows):
        return remote(ref.at[y, rows], ref.at[y, rows], xlo_s.at[i], xlo_r.at[i], near)

    fetch_x.wait()
    start(near_copy(0, xg, own_tile))
    fetch_dy.wait()
    start(near_copy(1, dyg, own_tile))

    def token_gather(i, ref, ups, downs):
        ring = Gather(
            y, ny, y_up, y_down, ups, downs,
            y_s.at[pl.ds(i * y_steps, y_steps)], y_r.at[pl.ds(i * y_steps, y_steps)], sent,
        )
        view = lambda q: ref.at[q, mine]

        def share(q):
            start(remote(ref.at[q, mine], ref.at[q, mine], sib_s.at[i, q], sib_r.at[i, q], sibling))

        def shared(q):
            remote(ref.at[q, theirs], ref.at[q, theirs], sib_s.at[i, q], sib_r.at[i, q], sibling).wait_recv()

        return ring, view, share, shared

    def token_step(gather, step, matmul):
        ring, view, share, shared = gather
        if step == 0:
            here = [y]
        else:
            here = ring.arrive(step - 1, view)
        ring.send(step, view)
        for q in here:
            share(q)
        for q in here:
            shared(q)
            matmul(q)

    def pre_chunk(q):
        pre_p[q] = dot_plain(xg[q], wu[...])

    def gact_chunk(q):
        gact_p[q] = dot_right_t(dyg[q], wd[...])

    x_gather = token_gather(0, xg, y_long, y_short)
    dy_gather = token_gather(1, dyg, y_short, y_long)

    near_copy(0, xg, near_tile).wait_recv()
    fetch_wu.wait()
    for step in range(y_long + 1):
        token_step(x_gather, step, pre_chunk)

    def z_ring(kind, i, ups, downs):
        return kind(
            z, nz, z_up, z_down, ups, downs,
            z_s.at[pl.ds(i * z_steps, z_steps)], z_r.at[pl.ds(i * z_steps, z_steps)], sent,
        )

    pre_ring = z_ring(Scatter, 0, z_long, z_short).bind(lambda q: pre_p[q], pre_out, pre_in)
    gact_ring = z_ring(Scatter, 1, z_short, z_long).bind(lambda q: gact_p[q], gact_out, gact_in)
    act_ring = z_ring(Gather, 2, z_short, z_long)
    gpre_ring = z_ring(Gather, 3, z_long, z_short)

    def pair_copy(i):
        return remote(pair_out.at[i], pair_in.at[i], pair_s.at[i], pair_r.at[i], far)

    near_copy(1, dyg, near_tile).wait_recv()
    fetch_wd.wait()
    for step in range(max(z_long, y_long + 1)):
        if step < z_long:
            pre_ring.step(step)
        if step < y_long + 1:
            token_step(dy_gather, step, gact_chunk)
    pre = pre_ring.finish()
    pre_p[z] = pre
    pair_out[0] = pre.astype(bf16)
    start(pair_copy(0))

    act_view = lambda q: act.at[q]
    gpre_view = lambda q: gpre.at[q]

    def activate():
        pair_copy(0).wait_recv()
        u = pre_p[z] + pair_in[0].astype(f32)
        t = jnp.tanh(slope_c * (u + cubic_a * u * u * u))
        act[z] = (0.5 * u * (1.0 + t)).astype(bf16)
        slope[...] = 0.5 * (1.0 + t) + 0.5 * u * (1.0 - t * t) * slope_c * (
            1.0 + 3.0 * cubic_a * u * u
        )
        act_ring.send(0, act_view)

    act_done = 0
    for step in range(z_long):
        gact_ring.step(step)
        if step == 1:
            activate()
        if step > 1:
            act_ring.arrive(act_done, act_view)
            act_done += 1
            act_ring.send(act_done, act_view)
    if z_long < 2:
        activate()
    gact = gact_ring.finish()
    gact_p[z] = gact
    pair_out[1] = gact.astype(bf16)
    start(pair_copy(1))
    while act_done < z_long:
        act_ring.arrive(act_done, act_view)
        act_done += 1
        act_ring.send(act_done, act_view)
    pair_copy(1).wait_recv()
    gpre[z] = ((gact_p[z] + pair_in[1].astype(f32)) * slope[...]).astype(bf16)

    def sib_copy(q):
        return remote(sib_out.at[q], sib_in.at[q], gsib_s.at[q], gsib_r.at[q], sibling)

    def gin_chunk(q):
        gin_p[q] = dot_right_t(gpre[q], wu[...])
        sib_out[q] = gin_p[q, theirs]
        start(sib_copy(q))

    gpre_ring.send(0, gpre_view)
    gin_chunk(z)
    rows = wu.shape[0]
    tokens = nz * 4 * tile
    third = rows // 3

    def gd_block(i):
        cols = pl.ds(i * third, third)
        left = act[:, :, cols].reshape(tokens, third)
        gd[cols, :] = dot_left_t(left, dyg[...].reshape(tokens, rows)).astype(bf16)

    def gu_block(i):
        cols = pl.ds(i * third, third)
        left = xg[:, :, cols].reshape(tokens, third)
        gu[cols, :] = dot_left_t(left, gpre[...].reshape(tokens, rows)).astype(bf16)

    for step in range(z_long):
        if step < 3:
            gd_block(step)
        here = gpre_ring.arrive(step, gpre_view)
        gpre_ring.send(step + 1, gpre_view)
        for q in here:
            gin_chunk(q)
    for step in range(z_long, 3):
        gd_block(step)
    store_gd = pltpu.make_async_copy(gd, gd_out, local_sem.at[4])
    store_gd.start()

    arrived = []

    def gin_part(q):
        sib_copy(q).wait_recv()
        return gin_p[q, mine] + sib_in[q]

    gin_ring = Scatter(y, ny, y_up, y_down, y_long, y_short, gy_s, gy_r, sent).bind(gin_part, gin_o, gin_i)
    for step in range(y_long):
        gin_ring.step(step)
        if step < 3:
            gu_block(step)
    for step in range(y_long, 3):
        gu_block(step)
    store_gu = pltpu.make_async_copy(gu, gu_out, local_sem.at[5])
    store_gu.start()
    last_p = gin_ring.finish()
    gin_p[y, mine] = last_p
    ours = pl.ds(pl.multiple_of(core * (2 * tile) + x_lo * tile, tile), tile)
    away = pl.ds(pl.multiple_of(core * (2 * tile) + (1 - x_lo) * tile, tile), tile)
    last_out[...] = gin_p[y, away]
    last = remote(last_out, last_in, gx_s.at[0], gx_r.at[0], near)
    start(last)
    last.wait_recv()
    gin_out[...] = (gin_p[y, ours] + last_in[...]).astype(bf16)
    store_gd.wait()
    store_gu.wait()
    for copy in sent:
        copy.wait_send()


def solution(mesh):
    nz = mesh.shape["row"] // 2
    ny = mesh.shape["col"] // 2

    def per_device(tokens, w_up, w_down, grad_out):
        depth, hidden = w_up.shape
        chunk = 4 * tile
        any_space = pl.BlockSpec(memory_space=pl.ANY)
        vmem_space = pl.BlockSpec(memory_space=pltpu.VMEM)
        dma = pltpu.SemaphoreType.DMA
        ys, zs = ny - 1, nz - 1
        scratch = [
            pltpu.VMEM((ny, chunk, depth), bf16),
            pltpu.VMEM((ny, chunk, depth), bf16),
            pltpu.VMEM((depth, hidden), bf16),
            pltpu.VMEM((hidden, depth), bf16),
            pltpu.VMEM((nz, chunk, hidden), f32),
            pltpu.VMEM((nz, chunk, hidden), f32),
            pltpu.VMEM((zs, chunk, hidden), bf16),
            pltpu.VMEM((zs, chunk, hidden), bf16),
            pltpu.VMEM((zs, chunk, hidden), bf16),
            pltpu.VMEM((zs, chunk, hidden), bf16),
            pltpu.VMEM((2, chunk, hidden), bf16),
            pltpu.VMEM((2, chunk, hidden), bf16),
            pltpu.VMEM((chunk, hidden), f32),
            pltpu.VMEM((nz, chunk, hidden), bf16),
            pltpu.VMEM((nz, chunk, hidden), bf16),
            pltpu.VMEM((nz, chunk, depth), f32),
            pltpu.VMEM((ny, 2 * tile, depth), f32),
            pltpu.VMEM((ny, 2 * tile, depth), f32),
            pltpu.VMEM((ys, 2 * tile, depth), f32),
            pltpu.VMEM((ys, 2 * tile, depth), f32),
            pltpu.VMEM((tile, depth), f32),
            pltpu.VMEM((tile, depth), f32),
            pltpu.VMEM((depth, hidden), bf16),
            pltpu.VMEM((hidden, depth), bf16),
            dma((6,)),
            dma((2,)), dma((2,)),
            dma((2 * ys,)), dma((2 * ys,)),
            dma((2, ny)), dma((2, ny)),
            dma((4 * zs,)), dma((4 * zs,)),
            dma((2,)), dma((2,)),
            dma((ny,)), dma((ny,)),
            dma((ys,)), dma((ys,)),
            dma((1,)), dma((1,)),
        ]
        return pl.pallas_call(
            functools.partial(kernel, nz, ny),
            out_shape=(
                jax.ShapeDtypeStruct(tokens.shape, bf16),
                jax.ShapeDtypeStruct(w_up.shape, bf16),
                jax.ShapeDtypeStruct(w_down.shape, bf16),
            ),
            in_specs=[any_space] * 4,
            out_specs=(vmem_space, any_space, any_space),
            scratch_shapes=scratch,
            compiler_params=pltpu.CompilerParams(
                collective_id=0, has_side_effects=True, vmem_limit_bytes=48 * 1024 * 1024
            ),
            cost_estimate=pl.CostEstimate(
                flops=5 * 2 * 512 * 768 * 768, bytes_accessed=5_000_000, transcendentals=64 * 768
            ),
        )(tokens, w_up, w_down, grad_out)

    in_specs = (
        P(("dp", "col"), "row"),
        P("row", ("dp", "col")),
        P(("dp", "col"), "row"),
        P(("dp", "col"), "row"),
    )
    out_specs = (P(("dp", "col"), "row"), P("row", ("dp", "col")), P(("dp", "col"), "row"))
    return jax.shard_map(
        per_device, mesh=mesh, in_specs=in_specs, out_specs=out_specs, check_vma=False
    )
```

```python
import functools
import math

import jax
import jax.numpy as jnp
from jax import lax
from jax.experimental import pallas as pl
from jax.experimental.pallas import tpu as pltpu
from jax.sharding import PartitionSpec as P

slope_c = math.sqrt(2.0 / math.pi)
cubic_a = 0.044715
f32 = jnp.float32
bf16 = jnp.bfloat16
tile = 16


def dot_plain(left, right):
    return lax.dot_general(left, right, (((1,), (0,)), ((), ())), preferred_element_type=f32)


def dot_right_t(left, right):
    return lax.dot_general(left, right, (((1,), (1,)), ((), ())), preferred_element_type=f32)


def dot_left_t(left, right):
    return lax.dot_general(left, right, (((0,), (0,)), ((), ())), preferred_element_type=f32)


def remote(src, dst, send_sem, recv_sem, device):
    return pltpu.make_async_remote_copy(
        src_ref=src,
        dst_ref=dst,
        send_sem=send_sem,
        recv_sem=recv_sem,
        device_id=device,
        device_id_type=pl.DeviceIdType.MESH,
    )


class Ring:
    def __init__(self, place, size, up, down, ups, downs, send_sems, recv_sems, sent):
        self.place, self.size, self.sent = place, size, sent
        self.ways = ((1, ups, 0, up), (-1, downs, ups, down))
        self.send_sems, self.recv_sems = send_sems, recv_sems

    def at(self, offset):
        return lax.rem(self.place + (offset + self.size), self.size)


class Gather(Ring):
    def copy(self, way, step, view, received=False):
        sign, _, base, device = way
        q = self.at(-sign * (step + 1 if received else step))
        ref = view(q)
        slot = base + step
        return remote(ref, ref, self.send_sems.at[slot], self.recv_sems.at[slot], device)

    def send(self, step, view):
        for way in self.ways:
            if step < way[1]:
                copy = self.copy(way, step, view)
                copy.start()
                self.sent.append(copy)

    def arrive(self, step, view):
        here = []
        for way in self.ways:
            if step < way[1]:
                self.copy(way, step, view, received=True).wait_recv()
                here.append(self.at(-way[0] * (step + 1)))
        return here


class Scatter(Ring):
    def bind(self, part, out_slots, in_slots):
        self.part, self.out_slots, self.in_slots = part, out_slots, in_slots
        return self

    def copy(self, way, step):
        _, _, base, device = way
        slot = base + step
        return remote(
            self.out_slots.at[slot],
            self.in_slots.at[slot],
            self.send_sems.at[slot],
            self.recv_sems.at[slot],
            device,
        )

    def step(self, step):
        for way in self.ways:
            sign, hops, base, _ = way
            if step < hops:
                total = self.part(self.at(sign * (hops - step)))
                if step > 0:
                    self.copy(way, step - 1).wait_recv()
                    total = total + self.in_slots[base + step - 1].astype(f32)
                self.out_slots[base + step] = total.astype(self.out_slots.dtype)
                copy = self.copy(way, step)
                copy.start()
                self.sent.append(copy)

    def finish(self):
        total = self.part(self.place)
        for way in self.ways:
            _, hops, base, _ = way
            if hops > 0:
                self.copy(way, hops - 1).wait_recv()
                total = total + self.in_slots[base + hops - 1].astype(f32)
        return total


def kernel(
    nz, ny,
    x_in, wu_in, wd_in, dy_in,
    gin_out, gu, gd,
    xg, dyg, wu, wd, pre_p, gact_p,
    pre_out, pre_in, gact_out, gact_in,
    pair_out, pair_in, slope,
    act, gpre, gin_p, sib_in, near_in, last_in,
    local_sem, y_s, y_r, near_s, near_r, sib_s, sib_r, z_s, z_r, pair_s, pair_r,
    gsib_s, gsib_r, gnear_s, gnear_r, gy_s, gy_r,
):
    core = lax.axis_index("dp")
    row = lax.axis_index("row")
    col = lax.axis_index("col")
    z, x_hi = lax.div(row, 2), lax.rem(row, 2)
    x_lo, y = lax.div(col, ny), lax.rem(col, ny)
    sent = []

    def start(copy):
        copy.start()
        sent.append(copy)

    def y_peer(q):
        return {"col": x_lo * ny + q}

    def y_at(offset):
        return lax.rem(y + (offset + ny), ny)

    z_up = {"row": lax.rem(z + 1, nz) * 2 + x_hi}
    z_down = {"row": lax.rem(z + nz - 1, nz) * 2 + x_hi}
    far = {"row": z * 2 + (1 - x_hi)}
    near = {"col": (1 - x_lo) * ny + y}
    sibling = {"dp": 1 - core}

    mine = pl.ds(pl.multiple_of(core * (2 * tile), 2 * tile), 2 * tile)
    theirs = pl.ds(pl.multiple_of((1 - core) * (2 * tile), 2 * tile), 2 * tile)
    own_tile = pl.ds(pl.multiple_of(core * (2 * tile) + x_lo * tile, tile), tile)
    near_tile = pl.ds(pl.multiple_of(core * (2 * tile) + (1 - x_lo) * tile, tile), tile)

    fetch_x = pltpu.make_async_copy(x_in, xg.at[y, own_tile], local_sem.at[0])
    fetch_dy = pltpu.make_async_copy(dy_in, dyg.at[y, own_tile], local_sem.at[1])
    fetch_wu = pltpu.make_async_copy(wu_in, wu, local_sem.at[2])
    fetch_wd = pltpu.make_async_copy(wd_in, wd, local_sem.at[3])
    for copy in (fetch_x, fetch_dy, fetch_wu, fetch_wd):
        copy.start()

    barrier = pltpu.get_barrier_semaphore()
    others = [y_peer(y_at(d)) for d in range(1, ny)] + [near, z_up, z_down, far, sibling]
    for device in others:
        pl.semaphore_signal(barrier, inc=1, device_id=device, device_id_type=pl.DeviceIdType.MESH)
    pl.semaphore_wait(barrier, len(others))

    z_long, z_short = nz // 2, nz - 1 - nz // 2
    z_steps = nz - 1
    order = sorted(range(1, ny), key=lambda d: min(d, ny - d))

    def tile_copy(i, ref, d, q, device):
        view = ref.at[q, own_tile]
        return remote(view, view, y_s.at[i, d], y_r.at[i, d], device)

    def near_copy(i, ref, d, rows):
        view = ref.at[y_at(-d), rows]
        return remote(view, view, near_s.at[i, d], near_r.at[i, d], near)

    def core_copy(i, ref, d, rows):
        view = ref.at[y_at(-d), rows]
        return remote(view, view, sib_s.at[i, d], sib_r.at[i, d], sibling)

    def scatter_tile(i, ref):
        for d in reversed(order):
            start(tile_copy(i, ref, d, y, y_peer(y_at(d))))
        start(near_copy(i, ref, 0, own_tile))

    def pass_near(i, ref):
        for d in order:
            tile_copy(i, ref, d, y_at(-d), y_peer(y_at(d))).wait_recv()
            start(near_copy(i, ref, d, own_tile))

    def groups():
        steps = [[0]]
        for k in range(0, len(order), 2):
            steps.append(order[k : k + 2])
        return steps

    def pass_core(i, ref, ds):
        for d in ds:
            near_copy(i, ref, d, near_tile).wait_recv()
            start(core_copy(i, ref, d, mine))

    def multiply(i, ref, ds, dot, weights, out):
        for d in ds:
            core_copy(i, ref, d, theirs).wait_recv()
        left = [ref[y_at(-d)] for d in ds]
        left = left[0] if len(left) == 1 else jnp.concatenate(left, axis=0)
        product = dot(left, weights[...])
        for k, d in enumerate(ds):
            out[y_at(-d)] = product[k * 4 * tile : (k + 1) * 4 * tile]

    def spread(i, ref, dot, weights, out):
        before = None
        for ds in groups():
            pass_core(i, ref, ds)
            if before is not None:
                multiply(i, ref, before, dot, weights, out)
            before = ds
        multiply(i, ref, before, dot, weights, out)

    fetch_x.wait()
    scatter_tile(0, xg)
    fetch_dy.wait()
    scatter_tile(1, dyg)
    pass_near(0, xg)
    fetch_wu.wait()
    spread(0, xg, dot_plain, wu, pre_p)

    def z_ring(kind, i, ups, downs):
        return kind(
            z, nz, z_up, z_down, ups, downs,
            z_s.at[pl.ds(i * z_steps, z_steps)], z_r.at[pl.ds(i * z_steps, z_steps)], sent,
        )

    pre_ring = z_ring(Scatter, 0, z_long, z_short).bind(lambda q: pre_p[q], pre_out, pre_in)
    gact_ring = z_ring(Scatter, 1, z_short, z_long).bind(lambda q: gact_p[q], gact_out, gact_in)
    act_ring = z_ring(Gather, 2, z_short, z_long)
    gpre_ring = z_ring(Gather, 3, z_long, z_short)

    def pair_copy(i):
        return remote(pair_out.at[i], pair_in.at[i], pair_s.at[i], pair_r.at[i], far)

    pre_ring.step(0)
    pass_near(1, dyg)
    fetch_wd.wait()
    spread(1, dyg, dot_right_t, wd, gact_p)
    gact_ring.step(0)
    for step in range(1, z_long):
        pre_ring.step(step)
        gact_ring.step(step)
    pre = pre_ring.finish()
    pre_p[z] = pre
    pair_out[0] = pre.astype(bf16)
    start(pair_copy(0))
    gact = gact_ring.finish()
    gact_p[z] = gact
    pair_out[1] = gact.astype(bf16)
    start(pair_copy(1))

    act_view = lambda q: act.at[q]
    gpre_view = lambda q: gpre.at[q]
    pair_copy(0).wait_recv()
    u = pre_p[z] + pair_in[0].astype(f32)
    t = jnp.tanh(slope_c * (u + cubic_a * u * u * u))
    act[z] = (0.5 * u * (1.0 + t)).astype(bf16)
    act_ring.send(0, act_view)
    slope[...] = 0.5 * (1.0 + t) + 0.5 * u * (1.0 - t * t) * slope_c * (1.0 + 3.0 * cubic_a * u * u)
    pair_copy(1).wait_recv()
    gpre[z] = ((gact_p[z] + pair_in[1].astype(f32)) * slope[...]).astype(bf16)
    gpre_ring.send(0, gpre_view)

    def gin_core(q, rows):
        return remote(gin_p.at[q, rows], sib_in.at[q], gsib_s.at[q], gsib_r.at[q], sibling)

    def gin_near(q):
        return remote(gin_p.at[q, near_tile], near_in.at[q], gnear_s.at[q], gnear_r.at[q], near)

    def gin_owner(q, d):
        return remote(gin_p.at[q, own_tile], last_in.at[d], gy_s.at[d], gy_r.at[d], y_peer(q))

    def gin_first(q):
        gin_p[q] = dot_right_t(gpre[q], wu[...])
        start(gin_core(q, theirs))

    def gin_second(q):
        gin_core(q, theirs).wait_recv()
        gin_p[q, mine] = gin_p[q, mine] + sib_in[q]
        start(gin_near(q))

    def gin_third(q):
        gin_near(q).wait_recv()
        gin_p[q, own_tile] = gin_p[q, own_tile] + near_in[q]

        @pl.when(q != y)
        def _():
            gin_owner(q, lax.rem(q - y + ny, ny)).start()

    depth = wu.shape[0]
    tokens = nz * 4 * tile
    third = depth // 3

    def weight_block(i, left, right, out):
        cols = pl.ds(i * third, third)
        block = dot_left_t(left[:, :, cols].reshape(tokens, third), right[...].reshape(tokens, depth))
        out[cols, :] = block.astype(bf16)

    gin_first(z)
    one, two = [z], []
    for step in range(z_long):
        here = gpre_ring.arrive(step, gpre_view)
        gpre_ring.send(step + 1, gpre_view)
        act_ring.arrive(step, act_view)
        act_ring.send(step + 1, act_view)
        for q in one:
            gin_second(q)
        for q in here:
            gin_first(q)
        for q in two:
            gin_third(q)
        one, two = here, one
    weight_block(0, act, dyg, gd)
    for q in one:
        gin_second(q)
    for q in two:
        gin_third(q)
    weight_block(1, act, dyg, gd)
    weight_block(2, act, dyg, gd)
    weight_block(0, xg, gpre, gu)
    for q in one:
        gin_third(q)
    weight_block(1, xg, gpre, gu)
    weight_block(2, xg, gpre, gu)
    total = gin_p[y, own_tile]
    for d in order:
        gin_owner(y_at(d), d).wait_recv()
        total = total + last_in[d]
    gin_out[...] = total.astype(bf16)
    for d in order:
        gin_owner(y_at(d), d).wait_send()
    for copy in sent:
        copy.wait_send()


def solution(mesh):
    nz = mesh.shape["row"] // 2
    ny = mesh.shape["col"] // 2

    def per_device(tokens, w_up, w_down, grad_out):
        depth, hidden = w_up.shape
        chunk = 4 * tile
        hbm_space = pl.BlockSpec(memory_space=pltpu.HBM)
        vmem_space = pl.BlockSpec(memory_space=pltpu.VMEM)
        dma = pltpu.SemaphoreType.DMA
        zs = nz - 1
        scratch = [
            pltpu.VMEM((ny, chunk, depth), bf16),
            pltpu.VMEM((ny, chunk, depth), bf16),
            pltpu.VMEM((depth, hidden), bf16),
            pltpu.VMEM((hidden, depth), bf16),
            pltpu.VMEM((nz, chunk, hidden), f32),
            pltpu.VMEM((nz, chunk, hidden), f32),
            pltpu.VMEM((zs, chunk, hidden), bf16),
            pltpu.VMEM((zs, chunk, hidden), bf16),
            pltpu.VMEM((zs, chunk, hidden), bf16),
            pltpu.VMEM((zs, chunk, hidden), bf16),
            pltpu.VMEM((2, chunk, hidden), bf16),
            pltpu.VMEM((2, chunk, hidden), bf16),
            pltpu.VMEM((chunk, hidden), f32),
            pltpu.VMEM((nz, chunk, hidden), bf16),
            pltpu.VMEM((nz, chunk, hidden), bf16),
            pltpu.VMEM((nz, chunk, depth), f32),
            pltpu.VMEM((ny, 2 * tile, depth), f32),
            pltpu.VMEM((ny, tile, depth), f32),
            pltpu.VMEM((ny, tile, depth), f32),
            dma((4,)),
            dma((2, ny)), dma((2, ny)),
            dma((2, ny)), dma((2, ny)),
            dma((2, ny)), dma((2, ny)),
            dma((4 * zs,)), dma((4 * zs,)),
            dma((2,)), dma((2,)),
            dma((ny,)), dma((ny,)),
            dma((ny,)), dma((ny,)),
            dma((ny,)), dma((ny,)),
        ]
        return pl.pallas_call(
            functools.partial(kernel, nz, ny),
            out_shape=(
                pltpu.VMEM(tokens.shape, bf16),
                pltpu.VMEM(w_up.shape, bf16),
                pltpu.VMEM(w_down.shape, bf16),
            ),
            in_specs=[hbm_space] * 4,
            out_specs=(vmem_space, vmem_space, vmem_space),
            scratch_shapes=scratch,
            compiler_params=pltpu.CompilerParams(
                collective_id=0, has_side_effects=True, vmem_limit_bytes=60 * 1024 * 1024
            ),
            cost_estimate=pl.CostEstimate(
                flops=5 * 2 * 512 * 768 * 768, bytes_accessed=5_000_000, transcendentals=64 * 768
            ),
        )(tokens, w_up, w_down, grad_out)

    in_specs = (
        P(("dp", "col"), "row"),
        P("row", ("dp", "col")),
        P(("dp", "col"), "row"),
        P(("dp", "col"), "row"),
    )
    out_specs = (P(("dp", "col"), "row"), P("row", ("dp", "col")), P(("dp", "col"), "row"))
    return jax.shard_map(
        per_device, mesh=mesh, in_specs=in_specs, out_specs=out_specs, check_vma=False
    )
```

```python
import functools
import math

import jax
import jax.numpy as jnp
from jax import lax
from jax.experimental import pallas as pl
from jax.experimental.pallas import tpu as pltpu
from jax.sharding import PartitionSpec as P

slope_c = math.sqrt(2.0 / math.pi)
cubic_a = 0.044715
f32 = jnp.float32
bf16 = jnp.bfloat16
tile = 16


def dot_plain(left, right):
    return lax.dot_general(left, right, (((1,), (0,)), ((), ())), preferred_element_type=f32)


def dot_right_t(left, right):
    return lax.dot_general(left, right, (((1,), (1,)), ((), ())), preferred_element_type=f32)


def dot_left_t(left, right):
    return lax.dot_general(left, right, (((0,), (0,)), ((), ())), preferred_element_type=f32)


def remote(src, dst, send_sem, recv_sem, device):
    return pltpu.make_async_remote_copy(
        src_ref=src,
        dst_ref=dst,
        send_sem=send_sem,
        recv_sem=recv_sem,
        device_id=device,
        device_id_type=pl.DeviceIdType.MESH,
    )


class Row:
    def __init__(self, nz, z, x_hi, reach, send_sems, recv_sems, sent):
        self.nz, self.z, self.x_hi, self.reach, self.sent = nz, z, x_hi, reach, sent
        self.send_sems, self.recv_sems = send_sems, recv_sems

    def at(self, up):
        return lax.rem(self.z + (up + self.nz), self.nz)

    def side(self, other):
        return 1 - self.x_hi if other else self.x_hi

    def device(self, up, other):
        return {"row": self.at(up) * 2 + self.side(other)}

    def half(self, other):
        rows = 2 * tile
        return pl.ds(pl.multiple_of(self.side(other) * rows, rows), rows)

    def hops(self, sign):
        behind = range(self.reach[sign] - 2, 0, -1)
        return [(k, other) for k in behind for other in (1, 0)] + [(0, 1)]


class Scatter(Row):
    def bind(self, terms, rounded, middle, slots):
        self.terms, self.rounded, self.middle, self.slots = terms, rounded, middle, slots
        self.names = [("mid", s, k, o) for s in (1, -1) for k, o in self.hops(s)]
        self.names += [("end", s, 1, o) for s in (1, -1) for o in (1, 0)] + [("end", 0, 0, 1)]
        self.names += [("two", 1, 2, 0), ("two", -1, 2, 0)]
        return self

    def copy(self, name):
        kind, sign, k, other = name
        slot = self.names.index(name)
        if kind == "two":
            src = self.middle.at[0 if sign > 0 else 1]
        else:
            behind = 2 if kind == "mid" else 0
            src = self.rounded.at[self.at(-sign * (behind + k)), self.half(other)]
        return remote(
            src, self.slots.at[slot], self.send_sems.at[slot], self.recv_sems.at[slot],
            self.device(-sign * k, other),
        )

    def start(self, name):
        copy = self.copy(name)
        copy.start()
        self.sent.append(copy)

    def take(self, name):
        self.copy(name).wait_recv()
        return self.slots[self.names.index(name)].astype(f32)

    def begin(self):
        for kind in ("mid", "end"):
            for name in self.names:
                if name[0] == kind:
                    self.start(name)

    def relay(self):
        for sign in (1, -1):
            total = self.terms[self.at(-2 * sign), self.half(0)]
            for k, other in reversed(self.hops(sign)):
                total = total + self.take(("mid", sign, k, other))
            self.middle[0 if sign > 0 else 1] = total.astype(bf16)
            self.start(("two", sign, 2, 0))

    def finish(self):
        total = self.terms[self.z, self.half(0)]
        for name in self.names:
            if name[0] == "end":
                total = total + self.take(name)
        for sign in (1, -1):
            total = total + self.take(("two", sign, 2, 0))
        return total


class Gather(Row):
    def bind(self, ref):
        self.ref = ref
        self.near = [("far", 0, 0, 1)] + [("one", s, 1, o) for s in (1, -1) for o in (1, 0)]
        self.two = [("two", 1, 2, 0), ("two", -1, 2, 0)]
        self.late = [("fwd", s, k, o) for s in (1, -1) for k, o in self.hops(s)]
        self.names = self.two + self.near + self.late
        return self

    def copy(self, name, received=False):
        kind, sign, k, other = name
        slot = self.names.index(name)
        behind = 2 if kind == "fwd" else 0
        if received:
            view = self.ref.at[self.at(-sign * (behind + k)), self.half(other)]
        else:
            view = self.ref.at[self.at(-sign * behind), self.half(0)]
        return remote(
            view, view, self.send_sems.at[slot], self.recv_sems.at[slot], self.device(sign * k, other)
        )

    def start(self, name):
        copy = self.copy(name)
        copy.start()
        self.sent.append(copy)

    def begin(self):
        for name in self.two + self.near:
            self.start(name)

    def relay(self):
        for name in self.two:
            self.copy(name, received=True).wait_recv()
            for late in self.late:
                if late[1] == name[1]:
                    self.start(late)

    def arrive(self, names):
        for name in names:
            self.copy(name, received=True).wait_recv()


def kernel(
    nz, ny,
    x_in, wu_in, wd_in, dy_in,
    gin_out, gu, gd,
    xg, dyg, wu, wd, pre_p, gact_p,
    pre_b, gact_b, middle, slots, slope,
    act, gpre, gin_p, sib_in, near_o, near_in, last_o, last_in,
    local_sem, y_s, y_r, near_s, near_r, sib_s, sib_r, z_s, z_r,
    gsib_s, gsib_r, gnear_s, gnear_r, gy_s, gy_r,
):
    core = lax.axis_index("dp")
    row = lax.axis_index("row")
    col = lax.axis_index("col")
    z, x_hi = lax.div(row, 2), lax.rem(row, 2)
    x_lo, y = lax.div(col, ny), lax.rem(col, ny)
    sent = []

    def start(copy):
        copy.start()
        sent.append(copy)

    def y_peer(q):
        return {"col": x_lo * ny + q}

    def y_at(offset):
        return lax.rem(y + (offset + ny), ny)

    near = {"col": (1 - x_lo) * ny + y}
    sibling = {"dp": 1 - core}

    mine = pl.ds(pl.multiple_of(core * (2 * tile), 2 * tile), 2 * tile)
    theirs = pl.ds(pl.multiple_of((1 - core) * (2 * tile), 2 * tile), 2 * tile)
    own_tile = pl.ds(pl.multiple_of(core * (2 * tile) + x_lo * tile, tile), tile)
    near_tile = pl.ds(pl.multiple_of(core * (2 * tile) + (1 - x_lo) * tile, tile), tile)

    fetch_x = pltpu.make_async_copy(x_in, xg.at[y, own_tile], local_sem.at[0])
    fetch_dy = pltpu.make_async_copy(dy_in, dyg.at[y, own_tile], local_sem.at[1])
    fetch_wu = pltpu.make_async_copy(wu_in, wu, local_sem.at[2])
    fetch_wd = pltpu.make_async_copy(wd_in, wd, local_sem.at[3])
    for copy in (fetch_x, fetch_dy, fetch_wu, fetch_wd):
        copy.start()

    barrier = pltpu.get_barrier_semaphore()
    place = Row(nz, z, x_hi, {}, None, None, None)
    others = [y_peer(y_at(d)) for d in range(1, ny)] + [near, sibling, place.device(0, 1)]
    others += [place.device(up, other) for up in (1, -1, 2, -2) for other in (0, 1)]
    for device in others:
        pl.semaphore_signal(barrier, inc=1, device_id=device, device_id_type=pl.DeviceIdType.MESH)
    pl.semaphore_wait(barrier, len(others))

    z_long, z_short = nz // 2, nz - 1 - nz // 2
    order = sorted(range(1, ny), key=lambda d: min(d, ny - d))

    def tile_copy(i, ref, d, q, device):
        view = ref.at[q, own_tile]
        return remote(view, view, y_s.at[i, d], y_r.at[i, d], device)

    def near_copy(i, ref, d, rows):
        view = ref.at[y_at(-d), rows]
        return remote(view, view, near_s.at[i, d], near_r.at[i, d], near)

    def core_copy(i, ref, d, rows):
        view = ref.at[y_at(-d), rows]
        return remote(view, view, sib_s.at[i, d], sib_r.at[i, d], sibling)

    def scatter_tile(i, ref):
        for d in reversed(order):
            start(tile_copy(i, ref, d, y, y_peer(y_at(d))))
        start(near_copy(i, ref, 0, own_tile))

    def pass_near(i, ref):
        for d in order:
            tile_copy(i, ref, d, y_at(-d), y_peer(y_at(d))).wait_recv()
            start(near_copy(i, ref, d, own_tile))

    def groups():
        steps = [[0]]
        for k in range(0, len(order), 2):
            steps.append(order[k : k + 2])
        return steps

    def pass_core(i, ref, ds):
        for d in ds:
            near_copy(i, ref, d, near_tile).wait_recv()
            start(core_copy(i, ref, d, mine))

    def multiply(i, ref, ds, dot, weights, out, rounded):
        for d in ds:
            core_copy(i, ref, d, theirs).wait_recv()
        left = [ref[y_at(-d)] for d in ds]
        left = left[0] if len(left) == 1 else jnp.concatenate(left, axis=0)
        product = dot(left, weights[...])
        for k, d in enumerate(ds):
            block = product[k * 4 * tile : (k + 1) * 4 * tile]
            out[y_at(-d)] = block
            rounded[y_at(-d)] = block.astype(bf16)

    def spread(i, ref, dot, weights, out, rounded):
        before = None
        for ds in groups():
            pass_core(i, ref, ds)
            if before is not None:
                multiply(i, ref, before, dot, weights, out, rounded)
            before = ds
        multiply(i, ref, before, dot, weights, out, rounded)

    fetch_x.wait()
    scatter_tile(0, xg)
    fetch_dy.wait()
    scatter_tile(1, dyg)
    pass_near(0, xg)
    pass_near(1, dyg)
    fetch_wu.wait()
    spread(0, xg, dot_plain, wu, pre_p, pre_b)

    def on_row(kind, i, ups, downs):
        return kind(nz, z, x_hi, {1: ups, -1: downs}, z_s.at[i], z_r.at[i], sent)

    pre_sum = on_row(Scatter, 0, z_long, z_short).bind(pre_p, pre_b, middle.at[0], slots.at[0])
    gact_sum = on_row(Scatter, 1, z_short, z_long).bind(gact_p, gact_b, middle.at[1], slots.at[1])
    act_all = on_row(Gather, 2, z_short, z_long).bind(act)
    gpre_all = on_row(Gather, 3, z_long, z_short).bind(gpre)
    block = place.half(0)

    pre_sum.begin()
    fetch_wd.wait()
    spread(1, dyg, dot_right_t, wd, gact_p, gact_b)
    gact_sum.begin()
    pre_sum.relay()
    gact_sum.relay()
    u = pre_sum.finish()
    t = jnp.tanh(slope_c * (u + cubic_a * u * u * u))
    act[z, block] = (0.5 * u * (1.0 + t)).astype(bf16)
    slope[...] = 0.5 * (1.0 + t) + 0.5 * u * (1.0 - t * t) * slope_c * (1.0 + 3.0 * cubic_a * u * u)
    gpre[z, block] = (gact_sum.finish() * slope[...]).astype(bf16)
    gpre_all.begin()

    def gin_core(q, rows):
        return remote(gin_p.at[q, rows], sib_in.at[q], gsib_s.at[q], gsib_r.at[q], sibling)

    def gin_near(q):
        return remote(near_o.at[q], near_in.at[q], gnear_s.at[q], gnear_r.at[q], near)

    def gin_owner(q, d):
        return remote(last_o.at[q], last_in.at[d], gy_s.at[d], gy_r.at[d], y_peer(q))

    def gin_first(group):
        product = dot_right_t(jnp.concatenate([gpre[q] for q in group], axis=0), wu[...])
        for k, q in enumerate(group):
            gin_p[q] = product[k * 4 * tile : (k + 1) * 4 * tile]
            start(gin_core(q, theirs))

    def gin_second(q):
        gin_core(q, theirs).wait_recv()
        gin_p[q, mine] = gin_p[q, mine] + sib_in[q]
        near_o[q] = gin_p[q, near_tile].astype(bf16)
        start(gin_near(q))

    def gin_third(q):
        gin_near(q).wait_recv()
        total = gin_p[q, own_tile] + near_in[q].astype(f32)
        gin_p[q, own_tile] = total
        last_o[q] = total.astype(bf16)

        @pl.when(q != y)
        def _():
            gin_owner(q, lax.rem(q - y + ny, ny)).start()

    depth = wu.shape[0]
    tokens = nz * 4 * tile
    third = depth // 3

    def weight_block(i, left, right, out):
        cols = pl.ds(i * third, third)
        block = dot_left_t(left[:, :, cols].reshape(tokens, third), right[...].reshape(tokens, depth))
        out[cols, :] = block.astype(bf16)

    early = [z] + [place.at(up) for up in (1, -1)]
    late = [place.at(up) for up in (2, -2, 3, -3, 4)]
    gpre_all.relay()
    act_all.begin()
    gpre_all.arrive(gpre_all.near)
    gin_first(early)
    for q in early:
        gin_second(q)
    gpre_all.arrive(gpre_all.late)
    gin_first(late[:2])
    gin_first(late[2:])
    act_all.relay()
    for q in early:
        gin_third(q)
    for q in late:
        gin_second(q)
    weight_block(0, xg, gpre, gu)
    weight_block(1, xg, gpre, gu)
    weight_block(2, xg, gpre, gu)
    for q in late:
        gin_third(q)
    act_all.arrive(act_all.near + act_all.late)
    weight_block(0, act, dyg, gd)
    weight_block(1, act, dyg, gd)
    weight_block(2, act, dyg, gd)
    total = gin_p[y, own_tile]
    for d in order:
        gin_owner(y_at(d), d).wait_recv()
        total = total + last_in[d].astype(f32)
    gin_out[...] = total.astype(bf16)
    for d in order:
        gin_owner(y_at(d), d).wait_send()
    for copy in sent:
        copy.wait_send()


def solution(mesh):
    nz = mesh.shape["row"] // 2
    ny = mesh.shape["col"] // 2

    def per_device(tokens, w_up, w_down, grad_out):
        depth, hidden = w_up.shape
        chunk = 4 * tile
        hbm_space = pl.BlockSpec(memory_space=pltpu.HBM)
        vmem_space = pl.BlockSpec(memory_space=pltpu.VMEM)
        dma = pltpu.SemaphoreType.DMA
        scratch = [
            pltpu.VMEM((ny, chunk, depth), bf16),
            pltpu.VMEM((ny, chunk, depth), bf16),
            pltpu.VMEM((depth, hidden), bf16),
            pltpu.VMEM((hidden, depth), bf16),
            pltpu.VMEM((nz, chunk, hidden), f32),
            pltpu.VMEM((nz, chunk, hidden), f32),
            pltpu.VMEM((nz, chunk, hidden), bf16),
            pltpu.VMEM((nz, chunk, hidden), bf16),
            pltpu.VMEM((2, 2, 2 * tile, hidden), bf16),
            pltpu.VMEM((2, 2 * nz - 1, 2 * tile, hidden), bf16),
            pltpu.VMEM((2 * tile, hidden), f32),
            pltpu.VMEM((nz, chunk, hidden), bf16),
            pltpu.VMEM((nz, chunk, hidden), bf16),
            pltpu.VMEM((nz, chunk, depth), f32),
            pltpu.VMEM((ny, 2 * tile, depth), f32),
            pltpu.VMEM((ny, tile, depth), bf16),
            pltpu.VMEM((ny, tile, depth), bf16),
            pltpu.VMEM((ny, tile, depth), bf16),
            pltpu.VMEM((ny, tile, depth), bf16),
            dma((4,)),
            dma((2, ny)), dma((2, ny)),
            dma((2, ny)), dma((2, ny)),
            dma((2, ny)), dma((2, ny)),
            dma((4, 2 * nz - 1)), dma((4, 2 * nz - 1)),
            dma((ny,)), dma((ny,)),
            dma((ny,)), dma((ny,)),
            dma((ny,)), dma((ny,)),
        ]
        return pl.pallas_call(
            functools.partial(kernel, nz, ny),
            out_shape=(
                pltpu.VMEM(tokens.shape, bf16),
                pltpu.VMEM(w_up.shape, bf16),
                pltpu.VMEM(w_down.shape, bf16),
            ),
            in_specs=[hbm_space] * 4,
            out_specs=(vmem_space, vmem_space, vmem_space),
            scratch_shapes=scratch,
            compiler_params=pltpu.CompilerParams(
                collective_id=0, has_side_effects=True, vmem_limit_bytes=60 * 1024 * 1024
            ),
            cost_estimate=pl.CostEstimate(
                flops=5 * 2 * 512 * 768 * 768, bytes_accessed=5_000_000, transcendentals=64 * 768
            ),
        )(tokens, w_up, w_down, grad_out)

    in_specs = (
        P(("dp", "col"), "row"),
        P("row", ("dp", "col")),
        P(("dp", "col"), "row"),
        P(("dp", "col"), "row"),
    )
    out_specs = (P(("dp", "col"), "row"), P("row", ("dp", "col")), P(("dp", "col"), "row"))
    return jax.shard_map(
        per_device, mesh=mesh, in_specs=in_specs, out_specs=out_specs, check_vma=False
    )
```

```python
import functools
import math

import jax
import jax.numpy as jnp
from jax import lax
from jax.experimental import pallas as pl
from jax.experimental.pallas import tpu as pltpu
from jax.sharding import PartitionSpec as P

slope_c = math.sqrt(2.0 / math.pi)
cubic_a = 0.044715
f32 = jnp.float32
bf16 = jnp.bfloat16
tile = 16


def dot_plain(left, right):
    return lax.dot_general(left, right, (((1,), (0,)), ((), ())), preferred_element_type=f32)


def dot_left_t(left, right):
    return lax.dot_general(left, right, (((0,), (0,)), ((), ())), preferred_element_type=f32)


def remote(src, dst, send_sem, recv_sem, device):
    return pltpu.make_async_remote_copy(
        src_ref=src,
        dst_ref=dst,
        send_sem=send_sem,
        recv_sem=recv_sem,
        device_id=device,
        device_id_type=pl.DeviceIdType.MESH,
    )


class Row:
    def __init__(self, nz, z, x_hi, reach, send_sems, recv_sems, sent):
        self.nz, self.z, self.x_hi, self.reach, self.sent = nz, z, x_hi, reach, sent
        self.send_sems, self.recv_sems = send_sems, recv_sems

    def at(self, up):
        return lax.rem(self.z + (up + self.nz), self.nz)

    def side(self, other):
        return 1 - self.x_hi if other else self.x_hi

    def device(self, up, other):
        return {"row": self.at(up) * 2 + self.side(other)}

    def half(self, other):
        rows = 2 * tile
        return pl.ds(pl.multiple_of(self.side(other) * rows, rows), rows)

    def hops(self, sign):
        behind = range(self.reach[sign] - 2, 0, -1)
        return [(k, other) for k in behind for other in (1, 0)] + [(0, 1)]


class Scatter(Row):
    def bind(self, terms, rounded, middle, slots):
        self.terms, self.rounded, self.middle, self.slots = terms, rounded, middle, slots
        self.names = [("mid", s, k, o) for s in (1, -1) for k, o in self.hops(s)]
        self.names += [("end", s, 1, o) for s in (1, -1) for o in (1, 0)] + [("end", 0, 0, 1)]
        self.names += [("two", 1, 2, 0), ("two", -1, 2, 0)]
        return self

    def copy(self, name):
        kind, sign, k, other = name
        slot = self.names.index(name)
        if kind == "two":
            src = self.middle.at[0 if sign > 0 else 1]
        else:
            behind = 2 if kind == "mid" else 0
            src = self.rounded.at[self.at(-sign * (behind + k)), self.half(other)]
        return remote(
            src, self.slots.at[slot], self.send_sems.at[slot], self.recv_sems.at[slot],
            self.device(-sign * k, other),
        )

    def start(self, name):
        copy = self.copy(name)
        copy.start()
        self.sent.append(copy)

    def take(self, name):
        self.copy(name).wait_recv()
        return self.slots[self.names.index(name)].astype(f32)

    def begin(self):
        for name in self.names:
            if name[0] == "mid":
                self.start(name)

    def begin_near(self):
        for name in self.names:
            if name[0] == "end":
                self.start(name)

    def relay(self):
        for sign in (1, -1):
            total = self.terms[self.at(-2 * sign), self.half(0)]
            for k, other in reversed(self.hops(sign)):
                total = total + self.take(("mid", sign, k, other))
            self.middle[0 if sign > 0 else 1] = total.astype(bf16)
            self.start(("two", sign, 2, 0))

    def finish(self):
        total = self.terms[self.z, self.half(0)]
        for name in self.names:
            if name[0] == "end":
                total = total + self.take(name)
        for sign in (1, -1):
            total = total + self.take(("two", sign, 2, 0))
        return total


class Gather(Row):
    def bind(self, ref):
        self.ref = ref
        self.near = [("far", 0, 0, 1)] + [("one", s, 1, o) for s in (1, -1) for o in (1, 0)]
        self.two = [("two", 1, 2, 0), ("two", -1, 2, 0)]
        self.late = [("fwd", s, k, o) for s in (1, -1) for k, o in self.hops(s)]
        self.names = self.two + self.near + self.late
        return self

    def copy(self, name, received=False):
        kind, sign, k, other = name
        slot = self.names.index(name)
        behind = 2 if kind == "fwd" else 0
        if received:
            view = self.ref.at[self.at(-sign * (behind + k)), self.half(other)]
        else:
            view = self.ref.at[self.at(-sign * behind), self.half(0)]
        return remote(
            view, view, self.send_sems.at[slot], self.recv_sems.at[slot], self.device(sign * k, other)
        )

    def start(self, name):
        copy = self.copy(name)
        copy.start()
        self.sent.append(copy)

    def begin(self):
        for name in self.two + self.near:
            self.start(name)

    def relay(self):
        for name in self.two:
            self.copy(name, received=True).wait_recv()
            for late in self.late:
                if late[1] == name[1]:
                    self.start(late)

    def arrive(self, names):
        for name in names:
            self.copy(name, received=True).wait_recv()


def kernel(
    nz, ny,
    x_in, wu_in, wd_in, dy_in,
    gin_out, gu, gd,
    xg, dyg, wu, wd, wut, wdt, pre_p, gact_p,
    pre_b, gact_b, middle, slots, slope,
    act, gpre, gin_p, sib_in, near_o, near_in, last_o, last_in,
    local_sem, y_s, y_r, near_s, near_r, sib_s, sib_r, z_s, z_r,
    gsib_s, gsib_r, gnear_s, gnear_r, gy_s, gy_r,
):
    core = lax.axis_index("dp")
    row = lax.axis_index("row")
    col = lax.axis_index("col")
    z, x_hi = lax.div(row, 2), lax.rem(row, 2)
    x_lo, y = lax.div(col, ny), lax.rem(col, ny)
    sent = []

    def start(copy):
        copy.start()
        sent.append(copy)

    def y_peer(q):
        return {"col": x_lo * ny + q}

    def y_at(offset):
        return lax.rem(y + (offset + ny), ny)

    near = {"col": (1 - x_lo) * ny + y}
    sibling = {"dp": 1 - core}

    mine = pl.ds(pl.multiple_of(core * (2 * tile), 2 * tile), 2 * tile)
    theirs = pl.ds(pl.multiple_of((1 - core) * (2 * tile), 2 * tile), 2 * tile)
    own_tile = pl.ds(pl.multiple_of(core * (2 * tile) + x_lo * tile, tile), tile)
    near_tile = pl.ds(pl.multiple_of(core * (2 * tile) + (1 - x_lo) * tile, tile), tile)

    fetch_x = pltpu.make_async_copy(x_in, xg.at[y, own_tile], local_sem.at[0])
    fetch_dy = pltpu.make_async_copy(dy_in, dyg.at[y, own_tile], local_sem.at[1])
    fetch_wu = pltpu.make_async_copy(wu_in, wu, local_sem.at[2])
    fetch_wd = pltpu.make_async_copy(wd_in, wd, local_sem.at[3])
    for copy in (fetch_x, fetch_dy, fetch_wu, fetch_wd):
        copy.start()

    barrier = pltpu.get_barrier_semaphore()
    place = Row(nz, z, x_hi, {}, None, None, None)
    others = [y_peer(y_at(d)) for d in range(1, ny)] + [near, sibling, place.device(0, 1)]
    others += [place.device(up, other) for up in (1, -1, 2, -2) for other in (0, 1)]
    for device in others:
        pl.semaphore_signal(barrier, inc=1, device_id=device, device_id_type=pl.DeviceIdType.MESH)
    pl.semaphore_wait(barrier, len(others))

    z_long, z_short = nz // 2, nz - 1 - nz // 2
    order = sorted(range(1, ny), key=lambda d: min(d, ny - d))

    def tile_copy(i, ref, d, q, device):
        view = ref.at[q, own_tile]
        return remote(view, view, y_s.at[i, d], y_r.at[i, d], device)

    def near_copy(i, ref, d, rows):
        view = ref.at[y_at(-d), rows]
        return remote(view, view, near_s.at[i, d], near_r.at[i, d], near)

    def core_copy(i, ref, d, rows):
        view = ref.at[y_at(-d), rows]
        return remote(view, view, sib_s.at[i, d], sib_r.at[i, d], sibling)

    def scatter_tile(i, ref):
        for d in reversed(order):
            start(tile_copy(i, ref, d, y, y_peer(y_at(d))))
        start(near_copy(i, ref, 0, own_tile))

    def pass_near(i, ref):
        for d in order:
            tile_copy(i, ref, d, y_at(-d), y_peer(y_at(d))).wait_recv()
            start(near_copy(i, ref, d, own_tile))

    def groups():
        cut = len(order) // 2 + 1
        return [[0] + order[:cut], order[cut:]]

    def pass_core(i, ref, ds):
        for d in ds:
            near_copy(i, ref, d, near_tile).wait_recv()
            start(core_copy(i, ref, d, mine))

    def multiply(i, ref, ds, dot, weights, out, rounded):
        for d in ds:
            core_copy(i, ref, d, theirs).wait_recv()
        left = [ref[y_at(-d)] for d in ds]
        left = left[0] if len(left) == 1 else jnp.concatenate(left, axis=0)
        product = dot(left, weights[...])
        for k, d in enumerate(ds):
            block = product[k * 4 * tile : (k + 1) * 4 * tile]
            out[y_at(-d)] = block
            rounded[y_at(-d)] = block.astype(bf16)

    def spread(i, ref, dot, weights, out, rounded):
        before = None
        for ds in groups():
            pass_core(i, ref, ds)
            if before is not None:
                multiply(i, ref, before, dot, weights, out, rounded)
            before = ds
        multiply(i, ref, before, dot, weights, out, rounded)

    fetch_x.wait()
    scatter_tile(0, xg)
    fetch_dy.wait()
    scatter_tile(1, dyg)
    fetch_wd.wait()
    wdt[...] = wd[...].T
    fetch_wu.wait()
    wut[...] = wu[...].T
    pass_near(0, xg)
    pass_near(1, dyg)
    spread(0, xg, dot_plain, wu, pre_p, pre_b)

    def on_row(kind, i, ups, downs):
        return kind(nz, z, x_hi, {1: ups, -1: downs}, z_s.at[i], z_r.at[i], sent)

    pre_sum = on_row(Scatter, 0, z_long, z_short).bind(pre_p, pre_b, middle.at[0], slots.at[0])
    gact_sum = on_row(Scatter, 1, z_short, z_long).bind(gact_p, gact_b, middle.at[1], slots.at[1])
    act_all = on_row(Gather, 2, z_short, z_long).bind(act)
    gpre_all = on_row(Gather, 3, z_long, z_short).bind(gpre)
    block = place.half(0)

    pre_sum.begin()
    spread(1, dyg, dot_plain, wdt, gact_p, gact_b)
    gact_sum.begin()
    pre_sum.relay()
    pre_sum.begin_near()
    gact_sum.relay()
    gact_sum.begin_near()
    u = pre_sum.finish()
    t = jnp.tanh(slope_c * (u + cubic_a * u * u * u))
    act[z, block] = (0.5 * u * (1.0 + t)).astype(bf16)
    slope[...] = 0.5 * (1.0 + t) + 0.5 * u * (1.0 - t * t) * slope_c * (1.0 + 3.0 * cubic_a * u * u)
    gpre[z, block] = (gact_sum.finish() * slope[...]).astype(bf16)
    gpre_all.begin()

    def gin_core(q, rows):
        return remote(gin_p.at[q, rows], sib_in.at[q], gsib_s.at[q], gsib_r.at[q], sibling)

    def gin_near(q):
        return remote(near_o.at[q], near_in.at[q], gnear_s.at[q], gnear_r.at[q], near)

    def gin_owner(q, d):
        return remote(last_o.at[q], last_in.at[d], gy_s.at[d], gy_r.at[d], y_peer(q))

    def gin_first(group):
        product = dot_plain(jnp.concatenate([gpre[q] for q in group], axis=0), wut[...])
        for k, q in enumerate(group):
            gin_p[q] = product[k * 4 * tile : (k + 1) * 4 * tile]
            start(gin_core(q, theirs))

    def gin_second(q):
        gin_core(q, theirs).wait_recv()
        gin_p[q, mine] = gin_p[q, mine] + sib_in[q]
        near_o[q] = gin_p[q, near_tile].astype(bf16)
        start(gin_near(q))

    def gin_third(q):
        gin_near(q).wait_recv()
        total = gin_p[q, own_tile] + near_in[q].astype(f32)
        gin_p[q, own_tile] = total
        last_o[q] = total.astype(bf16)

        @pl.when(q != y)
        def _():
            gin_owner(q, lax.rem(q - y + ny, ny)).start()

    depth = wu.shape[0]
    tokens = nz * 4 * tile
    third = depth // 3

    def weight_block(i, left, right, out):
        cols = pl.ds(i * third, third)
        block = dot_left_t(left[:, :, cols].reshape(tokens, third), right[...].reshape(tokens, depth))
        out[cols, :] = block.astype(bf16)

    early = [z] + [place.at(up) for up in (1, -1)]
    late = [place.at(up) for up in (2, -2, 3, -3, 4)]
    gpre_all.relay()
    act_all.begin()
    gpre_all.arrive(gpre_all.near)
    gin_first(early)
    for q in early:
        gin_second(q)
    gpre_all.arrive(gpre_all.late)
    gin_first(late[:2])
    gin_first(late[2:])
    act_all.relay()
    for q in early:
        gin_third(q)
    for q in late:
        gin_second(q)
    weight_block(0, xg, gpre, gu)
    weight_block(1, xg, gpre, gu)
    weight_block(2, xg, gpre, gu)
    for q in late:
        gin_third(q)
    act_all.arrive(act_all.near + act_all.late)
    weight_block(0, act, dyg, gd)
    weight_block(1, act, dyg, gd)
    weight_block(2, act, dyg, gd)
    total = gin_p[y, own_tile]
    for d in order:
        gin_owner(y_at(d), d).wait_recv()
        total = total + last_in[d].astype(f32)
    gin_out[...] = total.astype(bf16)
    for d in order:
        gin_owner(y_at(d), d).wait_send()
    for copy in sent:
        copy.wait_send()


def solution(mesh):
    nz = mesh.shape["row"] // 2
    ny = mesh.shape["col"] // 2

    def per_device(tokens, w_up, w_down, grad_out):
        depth, hidden = w_up.shape
        chunk = 4 * tile
        hbm_space = pl.BlockSpec(memory_space=pltpu.HBM)
        vmem_space = pl.BlockSpec(memory_space=pltpu.VMEM)
        dma = pltpu.SemaphoreType.DMA
        scratch = [
            pltpu.VMEM((ny, chunk, depth), bf16),
            pltpu.VMEM((ny, chunk, depth), bf16),
            pltpu.VMEM((depth, hidden), bf16),
            pltpu.VMEM((hidden, depth), bf16),
            pltpu.VMEM((hidden, depth), bf16),
            pltpu.VMEM((depth, hidden), bf16),
            pltpu.VMEM((nz, chunk, hidden), f32),
            pltpu.VMEM((nz, chunk, hidden), f32),
            pltpu.VMEM((nz, chunk, hidden), bf16),
            pltpu.VMEM((nz, chunk, hidden), bf16),
            pltpu.VMEM((2, 2, 2 * tile, hidden), bf16),
            pltpu.VMEM((2, 2 * nz - 1, 2 * tile, hidden), bf16),
            pltpu.VMEM((2 * tile, hidden), f32),
            pltpu.VMEM((nz, chunk, hidden), bf16),
            pltpu.VMEM((nz, chunk, hidden), bf16),
            pltpu.VMEM((nz, chunk, depth), f32),
            pltpu.VMEM((ny, 2 * tile, depth), f32),
            pltpu.VMEM((ny, tile, depth), bf16),
            pltpu.VMEM((ny, tile, depth), bf16),
            pltpu.VMEM((ny, tile, depth), bf16),
            pltpu.VMEM((ny, tile, depth), bf16),
            dma((4,)),
            dma((2, ny)), dma((2, ny)),
            dma((2, ny)), dma((2, ny)),
            dma((2, ny)), dma((2, ny)),
            dma((4, 2 * nz - 1)), dma((4, 2 * nz - 1)),
            dma((ny,)), dma((ny,)),
            dma((ny,)), dma((ny,)),
            dma((ny,)), dma((ny,)),
        ]
        return pl.pallas_call(
            functools.partial(kernel, nz, ny),
            out_shape=(
                pltpu.VMEM(tokens.shape, bf16),
                pltpu.VMEM(w_up.shape, bf16),
                pltpu.VMEM(w_down.shape, bf16),
            ),
            in_specs=[hbm_space] * 4,
            out_specs=(vmem_space, vmem_space, vmem_space),
            scratch_shapes=scratch,
            compiler_params=pltpu.CompilerParams(
                collective_id=0, has_side_effects=True, vmem_limit_bytes=60 * 1024 * 1024
            ),
            cost_estimate=pl.CostEstimate(
                flops=5 * 2 * 512 * 768 * 768, bytes_accessed=5_000_000, transcendentals=64 * 768
            ),
        )(tokens, w_up, w_down, grad_out)

    in_specs = (
        P(("dp", "col"), "row"),
        P("row", ("dp", "col")),
        P(("dp", "col"), "row"),
        P(("dp", "col"), "row"),
    )
    out_specs = (P(("dp", "col"), "row"), P("row", ("dp", "col")), P(("dp", "col"), "row"))
    return jax.shard_map(
        per_device, mesh=mesh, in_specs=in_specs, out_specs=out_specs, check_vma=False
    )
```

```python
import functools
import math

import jax
import jax.numpy as jnp
from jax import lax
from jax.experimental import pallas as pl
from jax.experimental.pallas import tpu as pltpu
from jax.sharding import PartitionSpec as P

slope_c = math.sqrt(2.0 / math.pi)
cubic_a = 0.044715
f32 = jnp.float32
bf16 = jnp.bfloat16
tile = 16


def dot_plain(left, right):
    return lax.dot_general(left, right, (((1,), (0,)), ((), ())), preferred_element_type=f32)


def dot_left_t(left, right):
    return lax.dot_general(left, right, (((0,), (0,)), ((), ())), preferred_element_type=f32)


def remote(src, dst, send_sem, recv_sem, device):
    return pltpu.make_async_remote_copy(
        src_ref=src,
        dst_ref=dst,
        send_sem=send_sem,
        recv_sem=recv_sem,
        device_id=device,
        device_id_type=pl.DeviceIdType.MESH,
    )


class Row:
    def __init__(self, nz, z, x_hi, reach, send_sems, recv_sems, sent):
        self.nz, self.z, self.x_hi, self.reach, self.sent = nz, z, x_hi, reach, sent
        self.send_sems, self.recv_sems = send_sems, recv_sems

    def at(self, up):
        return lax.rem(self.z + (up + self.nz), self.nz)

    def side(self, other):
        return 1 - self.x_hi if other else self.x_hi

    def device(self, up, other):
        return {"row": self.at(up) * 2 + self.side(other)}

    def half(self, other):
        rows = 2 * tile
        return pl.ds(pl.multiple_of(self.side(other) * rows, rows), rows)

    def hops(self, sign):
        behind = range(self.reach[sign] - 2, 0, -1)
        return [(k, other) for k in behind for other in (1, 0)] + [(0, 1)]


class Scatter(Row):
    def bind(self, terms, rounded, middle, slots):
        self.terms, self.rounded, self.middle, self.slots = terms, rounded, middle, slots
        self.names = [("mid", s, k, o) for s in (1, -1) for k, o in self.hops(s)]
        self.names += [("end", s, 1, o) for s in (1, -1) for o in (1, 0)] + [("end", 0, 0, 1)]
        self.names += [("two", 1, 2, 0), ("two", -1, 2, 0)]
        return self

    def copy(self, name):
        kind, sign, k, other = name
        slot = self.names.index(name)
        if kind == "two":
            src = self.middle.at[0 if sign > 0 else 1]
        else:
            behind = 2 if kind == "mid" else 0
            src = self.rounded.at[self.at(-sign * (behind + k)), self.half(other)]
        return remote(
            src, self.slots.at[slot], self.send_sems.at[slot], self.recv_sems.at[slot],
            self.device(-sign * k, other),
        )

    def start(self, name):
        copy = self.copy(name)
        copy.start()
        self.sent.append(copy)

    def take(self, name):
        self.copy(name).wait_recv()
        return self.slots[self.names.index(name)].astype(f32)

    def begin(self):
        for name in self.names:
            if name[0] == "mid":
                self.start(name)

    def begin_near(self):
        for name in self.names:
            if name[0] == "end":
                self.start(name)

    def relay(self):
        for sign in (1, -1):
            total = self.terms[self.at(-2 * sign), self.half(0)]
            for k, other in reversed(self.hops(sign)):
                total = total + self.take(("mid", sign, k, other))
            self.middle[0 if sign > 0 else 1] = total.astype(bf16)
            self.start(("two", sign, 2, 0))

    def finish(self):
        total = self.terms[self.z, self.half(0)]
        for name in self.names:
            if name[0] == "end":
                total = total + self.take(name)
        for sign in (1, -1):
            total = total + self.take(("two", sign, 2, 0))
        return total


class Gather(Row):
    def bind(self, ref):
        self.ref = ref
        self.near = [("far", 0, 0, 1)] + [("one", s, 1, o) for s in (1, -1) for o in (1, 0)]
        self.two = [("two", 1, 2, 0), ("two", -1, 2, 0)]
        self.late = [("fwd", s, k, o) for s in (1, -1) for k, o in self.hops(s)]
        self.names = self.two + self.near + self.late
        return self

    def copy(self, name, received=False):
        kind, sign, k, other = name
        slot = self.names.index(name)
        behind = 2 if kind == "fwd" else 0
        if received:
            view = self.ref.at[self.at(-sign * (behind + k)), self.half(other)]
        else:
            view = self.ref.at[self.at(-sign * behind), self.half(0)]
        return remote(
            view, view, self.send_sems.at[slot], self.recv_sems.at[slot], self.device(sign * k, other)
        )

    def start(self, name):
        copy = self.copy(name)
        copy.start()
        self.sent.append(copy)

    def begin(self):
        for name in self.two + self.near:
            self.start(name)

    def relay(self):
        for name in self.two:
            self.copy(name, received=True).wait_recv()
            for late in self.late:
                if late[1] == name[1]:
                    self.start(late)

    def arrive(self, names):
        for name in names:
            self.copy(name, received=True).wait_recv()


def kernel(
    nz, ny,
    x_in, wu_in, wd_in, dy_in,
    gin_out, gu, gd,
    xg, dyg, wu, wd, wut, wdt, pre_p, gact_p,
    pre_b, gact_b, middle, slots, slope,
    act, gpre, gin_p, sib_in, near_o, near_in, last_o, last_in,
    local_sem, y_s, y_r, near_s, near_r, sib_s, sib_r, z_s, z_r,
    gsib_s, gsib_r, gnear_s, gnear_r, gy_s, gy_r,
):
    core = lax.axis_index("dp")
    row = lax.axis_index("row")
    col = lax.axis_index("col")
    z, x_hi = lax.div(row, 2), lax.rem(row, 2)
    x_lo, y = lax.div(col, ny), lax.rem(col, ny)
    sent = []

    def start(copy):
        copy.start()
        sent.append(copy)

    def y_peer(q):
        return {"col": x_lo * ny + q}

    def y_at(offset):
        return lax.rem(y + (offset + ny), ny)

    near = {"col": (1 - x_lo) * ny + y}
    sibling = {"dp": 1 - core}

    mine = pl.ds(pl.multiple_of(core * (2 * tile), 2 * tile), 2 * tile)
    theirs = pl.ds(pl.multiple_of((1 - core) * (2 * tile), 2 * tile), 2 * tile)
    own_tile = pl.ds(pl.multiple_of(core * (2 * tile) + x_lo * tile, tile), tile)
    near_tile = pl.ds(pl.multiple_of(core * (2 * tile) + (1 - x_lo) * tile, tile), tile)

    fetch_x = pltpu.make_async_copy(x_in, xg.at[y, own_tile], local_sem.at[0])
    fetch_dy = pltpu.make_async_copy(dy_in, dyg.at[y, own_tile], local_sem.at[1])
    fetch_wu = pltpu.make_async_copy(wu_in, wu, local_sem.at[2])
    fetch_wd = pltpu.make_async_copy(wd_in, wd, local_sem.at[3])
    for copy in (fetch_x, fetch_dy, fetch_wu, fetch_wd):
        copy.start()

    barrier = pltpu.get_barrier_semaphore()
    place = Row(nz, z, x_hi, {}, None, None, None)
    others = [y_peer(y_at(d)) for d in range(1, ny)] + [near, sibling, place.device(0, 1)]
    others += [place.device(up, other) for up in (1, -1, 2, -2) for other in (0, 1)]
    for device in others:
        pl.semaphore_signal(barrier, inc=1, device_id=device, device_id_type=pl.DeviceIdType.MESH)
    pl.semaphore_wait(barrier, len(others))

    z_long, z_short = nz // 2, nz - 1 - nz // 2
    order = sorted(range(1, ny), key=lambda d: min(d, ny - d))

    def tile_copy(i, ref, d, q, device):
        view = ref.at[q, own_tile]
        return remote(view, view, y_s.at[i, d], y_r.at[i, d], device)

    def near_copy(i, ref, d, rows):
        view = ref.at[y_at(-d), rows]
        return remote(view, view, near_s.at[i, d], near_r.at[i, d], near)

    def core_copy(i, ref, d, rows):
        view = ref.at[y_at(-d), rows]
        return remote(view, view, sib_s.at[i, d], sib_r.at[i, d], sibling)

    def scatter_tile(i, ref):
        for d in reversed(order):
            start(tile_copy(i, ref, d, y, y_peer(y_at(d))))
        start(near_copy(i, ref, 0, own_tile))

    def pass_near(i, ref):
        for d in order:
            tile_copy(i, ref, d, y_at(-d), y_peer(y_at(d))).wait_recv()
            start(near_copy(i, ref, d, own_tile))

    def groups():
        cut = len(order) // 2 + 1
        return [[0] + order[:cut], order[cut:]]

    def pass_core(i, ref, ds):
        for d in ds:
            near_copy(i, ref, d, near_tile).wait_recv()
            start(core_copy(i, ref, d, mine))

    def multiply(i, ref, ds, dot, weights, out, rounded):
        for d in ds:
            core_copy(i, ref, d, theirs).wait_recv()
        left = [ref[y_at(-d)] for d in ds]
        left = left[0] if len(left) == 1 else jnp.concatenate(left, axis=0)
        product = dot(left, weights[...])
        for k, d in enumerate(ds):
            block = product[k * 4 * tile : (k + 1) * 4 * tile]
            out[y_at(-d)] = block
            rounded[y_at(-d)] = block.astype(bf16)

    def spread(i, ref, dot, weights, out, rounded):
        before = None
        for ds in groups():
            pass_core(i, ref, ds)
            if before is not None:
                multiply(i, ref, before, dot, weights, out, rounded)
            before = ds
        multiply(i, ref, before, dot, weights, out, rounded)

    fetch_x.wait()
    scatter_tile(0, xg)
    fetch_dy.wait()
    scatter_tile(1, dyg)
    fetch_wd.wait()
    wdt[...] = wd[...].T
    fetch_wu.wait()
    wut[...] = wu[...].T
    pass_near(0, xg)
    pass_near(1, dyg)
    spread(0, xg, dot_plain, wu, pre_p, pre_b)

    def on_row(kind, i, ups, downs):
        return kind(nz, z, x_hi, {1: ups, -1: downs}, z_s.at[i], z_r.at[i], sent)

    pre_sum = on_row(Scatter, 0, z_long, z_short).bind(pre_p, pre_b, middle.at[0], slots.at[0])
    gact_sum = on_row(Scatter, 1, z_short, z_long).bind(gact_p, gact_b, middle.at[1], slots.at[1])
    act_all = on_row(Gather, 2, z_short, z_long).bind(act)
    gpre_all = on_row(Gather, 3, z_long, z_short).bind(gpre)
    block = place.half(0)

    pre_sum.begin()
    spread(1, dyg, dot_plain, wdt, gact_p, gact_b)
    gact_sum.begin()
    pre_sum.relay()
    pre_sum.begin_near()
    gact_sum.relay()
    gact_sum.begin_near()
    u = pre_sum.finish()
    t = jnp.tanh(slope_c * (u + cubic_a * u * u * u))
    act[z, block] = (0.5 * u * (1.0 + t)).astype(bf16)
    slope[...] = 0.5 * (1.0 + t) + 0.5 * u * (1.0 - t * t) * slope_c * (1.0 + 3.0 * cubic_a * u * u)
    gpre[z, block] = (gact_sum.finish() * slope[...]).astype(bf16)
    gpre_all.begin()

    def gin_core(q, rows):
        return remote(gin_p.at[q, rows], sib_in.at[q], gsib_s.at[q], gsib_r.at[q], sibling)

    def gin_near(q):
        return remote(near_o.at[q], near_in.at[q], gnear_s.at[q], gnear_r.at[q], near)

    def gin_owner(q, d):
        return remote(last_o.at[q], last_in.at[d], gy_s.at[d], gy_r.at[d], y_peer(q))

    def gin_first(group):
        product = dot_plain(jnp.concatenate([gpre[q] for q in group], axis=0), wut[...])
        for k, q in enumerate(group):
            gin_p[q] = product[k * 4 * tile : (k + 1) * 4 * tile]
            start(gin_core(q, theirs))

    def gin_second(q):
        gin_core(q, theirs).wait_recv()
        gin_p[q, mine] = gin_p[q, mine] + sib_in[q]
        near_o[q] = gin_p[q, near_tile].astype(bf16)
        start(gin_near(q))

    def gin_third(q):
        gin_near(q).wait_recv()
        total = gin_p[q, own_tile] + near_in[q].astype(f32)
        gin_p[q, own_tile] = total
        last_o[q] = total.astype(bf16)

        @pl.when(q != y)
        def _():
            gin_owner(q, lax.rem(q - y + ny, ny)).start()

    depth = wu.shape[0]
    tokens = nz * 4 * tile
    third = depth // 3

    def weight_block(i, left, right, out):
        cols = pl.ds(i * third, third)
        block = dot_left_t(left[:, :, cols].reshape(tokens, third), right[...].reshape(tokens, depth))
        out[cols, :] = block.astype(bf16)

    early = [z] + [place.at(up) for up in (1, -1)]
    late = [place.at(up) for up in (2, -2, 3, -3, 4)]
    gpre_all.relay()
    act_all.begin()
    gpre_all.arrive(gpre_all.near)
    gin_first(early)
    for q in early:
        gin_second(q)
    gpre_all.arrive(gpre_all.late)
    gin_first(late[:2])
    gin_first(late[2:])
    for q in late:
        gin_second(q)
    for q in early:
        gin_third(q)
    act_all.relay()
    weight_block(0, xg, gpre, gu)
    weight_block(1, xg, gpre, gu)
    weight_block(2, xg, gpre, gu)
    for q in late:
        gin_third(q)
    act_all.arrive(act_all.near + act_all.late)
    weight_block(0, act, dyg, gd)
    weight_block(1, act, dyg, gd)
    weight_block(2, act, dyg, gd)
    total = gin_p[y, own_tile]
    for d in order:
        gin_owner(y_at(d), d).wait_recv()
        total = total + last_in[d].astype(f32)
    gin_out[...] = total.astype(bf16)
    for d in order:
        gin_owner(y_at(d), d).wait_send()
    for copy in sent:
        copy.wait_send()


def solution(mesh):
    nz = mesh.shape["row"] // 2
    ny = mesh.shape["col"] // 2

    def per_device(tokens, w_up, w_down, grad_out):
        depth, hidden = w_up.shape
        chunk = 4 * tile
        hbm_space = pl.BlockSpec(memory_space=pltpu.HBM)
        vmem_space = pl.BlockSpec(memory_space=pltpu.VMEM)
        dma = pltpu.SemaphoreType.DMA
        scratch = [
            pltpu.VMEM((ny, chunk, depth), bf16),
            pltpu.VMEM((ny, chunk, depth), bf16),
            pltpu.VMEM((depth, hidden), bf16),
            pltpu.VMEM((hidden, depth), bf16),
            pltpu.VMEM((hidden, depth), bf16),
            pltpu.VMEM((depth, hidden), bf16),
            pltpu.VMEM((nz, chunk, hidden), f32),
            pltpu.VMEM((nz, chunk, hidden), f32),
            pltpu.VMEM((nz, chunk, hidden), bf16),
            pltpu.VMEM((nz, chunk, hidden), bf16),
            pltpu.VMEM((2, 2, 2 * tile, hidden), bf16),
            pltpu.VMEM((2, 2 * nz - 1, 2 * tile, hidden), bf16),
            pltpu.VMEM((2 * tile, hidden), f32),
            pltpu.VMEM((nz, chunk, hidden), bf16),
            pltpu.VMEM((nz, chunk, hidden), bf16),
            pltpu.VMEM((nz, chunk, depth), f32),
            pltpu.VMEM((ny, 2 * tile, depth), f32),
            pltpu.VMEM((ny, tile, depth), bf16),
            pltpu.VMEM((ny, tile, depth), bf16),
            pltpu.VMEM((ny, tile, depth), bf16),
            pltpu.VMEM((ny, tile, depth), bf16),
            dma((4,)),
            dma((2, ny)), dma((2, ny)),
            dma((2, ny)), dma((2, ny)),
            dma((2, ny)), dma((2, ny)),
            dma((4, 2 * nz - 1)), dma((4, 2 * nz - 1)),
            dma((ny,)), dma((ny,)),
            dma((ny,)), dma((ny,)),
            dma((ny,)), dma((ny,)),
        ]
        return pl.pallas_call(
            functools.partial(kernel, nz, ny),
            out_shape=(
                pltpu.VMEM(tokens.shape, bf16),
                pltpu.VMEM(w_up.shape, bf16),
                pltpu.VMEM(w_down.shape, bf16),
            ),
            in_specs=[hbm_space] * 4,
            out_specs=(vmem_space, vmem_space, vmem_space),
            scratch_shapes=scratch,
            compiler_params=pltpu.CompilerParams(
                collective_id=0, has_side_effects=True, vmem_limit_bytes=60 * 1024 * 1024
            ),
            cost_estimate=pl.CostEstimate(
                flops=5 * 2 * 512 * 768 * 768, bytes_accessed=5_000_000, transcendentals=64 * 768
            ),
        )(tokens, w_up, w_down, grad_out)

    in_specs = (
        P(("dp", "col"), "row"),
        P("row", ("dp", "col")),
        P(("dp", "col"), "row"),
        P(("dp", "col"), "row"),
    )
    out_specs = (P(("dp", "col"), "row"), P("row", ("dp", "col")), P(("dp", "col"), "row"))
    return jax.shard_map(
        per_device, mesh=mesh, in_specs=in_specs, out_specs=out_specs, check_vma=False
    )
```
